128 devices in a mesh: dp: 64 (over y_hi, x, z, core), tensor: 2 (over y_lo).
Axes of the slice: x: 4, y: 4 (y_hi: 2, y_lo: 2; y = y_hi * 2 + y_lo), z: 4, core: 2. Of those that a mesh axis runs over, the one named last changes fastest.
Arguments:
- queries: bfloat16 [2, 64, 256, 4096], P(None, 'dp', None, 'tensor'), may hold values from -160 to 160
- trace_kv: bfloat16 [2, 64, 256, 2, 512], P(None, 'dp', None, None, 'tensor'), may hold values from -4 to 4
- lengths: int32 [2, 64], P(None, 'dp'), may hold values from 32 to 256, as said below
- prompt_kv: bfloat16 [1024, 2, 512], P(('dp', 'tensor')), may hold values from -4 to 4
Outputs:
- attended: bfloat16 [2, 64, 256, 4096], P(None, 'dp', None, 'tensor')
The draws below stay inside these ranges and needn't reach their ends.
Inputs may be any that keep to these rules, and one draw needn't show every extreme that they name: lengths do not rise with rank (row-major order of the array); the first is 256 and the last is 32.
All inputs are finite; a program needn't handle non-finite values.
Results may differ from the reference program's by a relative error of at most 0.0045.
Values may be sent and summed in bfloat16 or wider, within the bound.
A program may use at most 64 MiB of HBM per device.

```python
import jax
import jax.numpy as jnp
from jax import lax

HQ = 32
G = 4
HEAD = 128
TRACE_SLOTS = 2
SLOT = 256
MINLEN = 32
TRACES = 128
PROMPT = 1024


def trace_keys(key):
    keys = jax.random.normal(key, (TRACE_SLOTS, TRACES // TRACE_SLOTS, SLOT, G, HEAD), jnp.float32)
    keys = jnp.clip(keys, -4.0, 4.0)
    positions = jnp.arange(SLOT)
    before = ((positions + 1) % 61 == 30)[None, None, :, None, None]
    return jnp.where(before, keys, keys)


def draw_trace_kv(key, part):
    keys = trace_keys(key)
    key = jax.random.fold_in(key, 7)
    values = jnp.clip(jax.random.normal(key, keys.shape, jnp.float32), -4.0, 4.0)
    target = keys.shape[:3] + (G * HEAD,)
    stacked = jnp.stack([keys.reshape(target), values.reshape(target)], axis=3)
    return stacked.astype(jnp.bfloat16)


def draw_queries(key, part):
    key = jax.random.fold_in(key, 5)
    per_group = HQ // G
    shape_full = (TRACE_SLOTS, TRACES // TRACE_SLOTS, SLOT, G, per_group, HEAD)
    queries = jnp.clip(jax.random.normal(key, shape_full, jnp.float32), -4.0, 4.0)
    return queries.reshape(TRACE_SLOTS, TRACES // TRACE_SLOTS, SLOT, HQ * HEAD).astype(jnp.bfloat16)


def draw_lengths(key, part):
    key = jax.random.fold_in(key, 3)
    drawn = jax.random.randint(key, (TRACES,), MINLEN, SLOT + 1, jnp.int32)
    ordered = -jnp.sort(-drawn)
    ordered = ordered.at[0].set(SLOT).at[TRACES - 1].set(MINLEN)
    return ordered.reshape(TRACE_SLOTS, TRACES // TRACE_SLOTS).astype(jnp.int32)


def block_scale(rng, extent, split, low, high):
    gain, own = 1.0, jax.random.fold_in(rng, 6)
    for dim, parts in split:
        steps = jnp.exp(jax.random.uniform(jax.random.fold_in(own, dim), (parts,), jnp.float32, low / len(split), high / len(split)))
        gain = gain * jnp.repeat(steps, extent[dim] // parts).reshape([-1 if axis == dim else 1 for axis in range(len(extent))])
    return gain


def bell_draw(rng, dims, width, limit, split=(), held_as=jnp.bfloat16):
    gain = block_scale(rng, dims, split, -0.22, 0.18) if split else 1.0
    array = jax.random.normal(rng, dims, jnp.float32) * width * gain
    return jnp.minimum(jnp.maximum(array, -limit), limit).astype(held_as)


def setup_inputs(seed: int = 0) -> dict:
    streams_of = jax.random.split(jax.random.key(seed), 5)
    queries = draw_queries(jax.random.fold_in(streams_of[4], 71), 0)
    trace_kv = draw_trace_kv(jax.random.fold_in(streams_of[4], 71), 0)
    lengths = draw_lengths(jax.random.fold_in(streams_of[4], 71), 0)
    prompt_kv = bell_draw(streams_of[3], (PROMPT, 2, G * HEAD), 1.0, 4.0, ((0, 128),))
    return {"queries": queries, "trace_kv": trace_kv, "lengths": lengths, "prompt_kv": prompt_kv}


def attend_trace(inputs, prompt_keys, prompt_values):
    query_rows, kv_rows, length = inputs
    per_group = HQ // G
    score_scale = 1.0 / jnp.sqrt(jnp.float32(HEAD))
    query_heads = query_rows.astype(jnp.float32).reshape(SLOT, G, per_group, HEAD)
    own_keys = kv_rows[:, 0].astype(jnp.float32).reshape(SLOT, G, HEAD)
    own_values = kv_rows[:, 1].astype(jnp.float32).reshape(SLOT, G, HEAD)
    prompt_scores = jnp.einsum('tgqd,sgd->gqts', query_heads, prompt_keys) * score_scale
    own_scores = jnp.einsum('tgqd,sgd->gqts', query_heads, own_keys) * score_scale
    positions = jnp.arange(SLOT, dtype=jnp.int32)
    allowed = (positions[None, :] <= positions[:, None]) & (positions[None, :] < length)
    own_scores = jnp.where(allowed, own_scores, -jnp.inf)
    scores = jnp.concatenate([prompt_scores, own_scores], axis=-1)
    top = lax.optimization_barrier(jnp.max(scores, axis=-1, keepdims=True))
    weights = jnp.exp(scores - top)
    totals = lax.optimization_barrier(jnp.sum(weights, axis=-1))
    rounded = lax.optimization_barrier(weights.astype(jnp.bfloat16)).astype(jnp.float32)
    values_all = jnp.concatenate([prompt_values, own_values], axis=0)
    summed = jnp.einsum('gqts,sgd->gqtd', rounded, values_all)
    result = summed / totals[..., None]
    result = jnp.transpose(result, (2, 0, 1, 3)).reshape(SLOT, HQ * HEAD)
    result = jnp.where(positions[:, None] < length, result, 0.0)
    return result.astype(jnp.bfloat16)

def reference(queries, trace_kv, lengths, prompt_kv):
    prompt_keys = prompt_kv[:, 0].astype(jnp.float32).reshape(PROMPT, G, HEAD)
    prompt_values = prompt_kv[:, 1].astype(jnp.float32).reshape(PROMPT, G, HEAD)
    flat_queries = queries.reshape(TRACES, SLOT, HQ * HEAD)
    flat_kv = trace_kv.reshape(TRACES, SLOT, 2, G * HEAD)
    flat_lengths = lengths.reshape(TRACES).astype(jnp.int32)

    def one_trace(inputs):
        return attend_trace(inputs, prompt_keys, prompt_values)
    results = lax.map(one_trace, (flat_queries, flat_kv, flat_lengths))
    return results.reshape(TRACE_SLOTS, TRACES // TRACE_SLOTS, SLOT, HQ * HEAD)
```

```python
import functools
import math

import jax
import jax.numpy as jnp
from jax import lax
from jax.experimental import pallas as pl
from jax.experimental.pallas import tpu as pltpu
from jax.sharding import PartitionSpec as P

MESH = pl.DeviceIdType.MESH
BF16 = jnp.bfloat16
F32 = jnp.float32
HEAD = 128
HEADS = 8
GROUPS = 2
SLOT = 256
PROMPT = 1024
TILE = 256
TOKENS = 64
ROWS = TOKENS * HEADS
SCALE = math.log2(math.e) / math.sqrt(HEAD)
NEG = -1e30


def turn(index, step):
    return lax.rem(index + step, 4)


def coordinates():
    dp, tensor = lax.axis_index("dp"), lax.axis_index("tensor")
    core = lax.rem(dp, 2)
    z = lax.rem(lax.div(dp, 2), 4)
    x = lax.rem(lax.div(dp, 8), 4)
    y = lax.div(dp, 32) * 2 + tensor
    return x, y, z, core


def device(x, y, z, core):
    return (((lax.div(y, 2) * 4 + x) * 4 + z) * 2 + core, lax.rem(y, 2))


def ring_hops(step):
    return min(step, 4 - step)


def remote(src, dst, send, recv, target):
    return pltpu.make_async_remote_copy(
        src_ref=src, dst_ref=dst, send_sem=send, recv_sem=recv, device_id=target, device_id_type=MESH
    )


def landed(ref, sem):
    pltpu.make_async_copy(ref, ref, sem).wait()


def gather_kernel(shard, out, kv, other, stage, s0, r0, s1, r1, s2, r2, s3, r3):
    x, y, z, core = coordinates()
    tensor = lax.rem(y, 2)
    outer = jnp.where(core == 0, z, x)
    inner = jnp.where(core == 0, x, z)

    def place(outer_, y_, inner_):
        return device(
            jnp.where(core == 0, inner_, outer_), y_, jnp.where(core == 0, outer_, inner_), core
        )

    partner = device(x, y, z, 1 - core)
    plane = [(dy, d) for dy in range(4) for d in range(4) if dy or d]
    plane.sort(key=lambda step: -ring_hops(step[0]) - ring_hops(step[1]))
    plane_devices = [place(outer, turn(y, dy), turn(inner, d)) for dy, d in plane]
    line_devices = {d: place(turn(outer, d), y, inner) for d in (1, 2, 3)}
    peers = plane_devices + list(line_devices.values()) + [partner]
    barrier = pltpu.get_barrier_semaphore()
    for peer in peers:
        pl.semaphore_signal(barrier, inc=1, device_id=peer, device_id_type=MESH)
    pl.semaphore_wait(barrier, len(peers))

    remote(shard.at[1 - core], other, s0.at[0], r0.at[0], partner).start()
    landed(other, r0.at[0])
    mine, theirs = shard[core], other[...]
    stage[:, 0] = jnp.concatenate([mine[:, 0:8], theirs[:, 0:8]], 1)
    stage[:, 1] = jnp.concatenate([mine[:, 8:16], theirs[:, 8:16]], 1)
    slot = inner * 4 + y
    kv[core, outer, :, slot] = stage[tensor]
    for (dy, _), target in zip(plane, plane_devices):
        to = lax.rem(turn(y, dy), 2)
        remote(stage.at[to], kv.at[core, outer, :, slot], s1.at[0], r1.at[0], target).start()
    landed(kv.at[core, outer, :, 0:15], r1.at[0])
    block = kv.at[core, outer]
    for d in (1, 3, 2):
        remote(block, block, s2.at[d], r2.at[d], line_devices[d]).start()
    remote(block, block, s3.at[0], r3.at[0], partner).start()
    for d in (1, 3, 2):
        block = kv.at[core, turn(outer, 4 - d)]
        landed(block, r2.at[d])
        remote(block, block, s3.at[d], r3.at[d], partner).start()
    for d in range(4):
        landed(kv.at[1 - core, 0], r3.at[d])
    landed(other, s0.at[0])
    landed(kv.at[core, outer, :, 0:15], s1.at[0])
    for d in range(4):
        if d:
            landed(block, s2.at[d])
        landed(block, s3.at[d])
    out[...] = kv[...]


def gather(prompt):
    shard = prompt.reshape(8, 2, 2, 2, HEAD).transpose(3, 2, 1, 0, 4).reshape(2, 2, 16, HEAD)
    vmem, dma = pltpu.VMEM, pltpu.SemaphoreType.DMA
    shape = (GROUPS, 4, 2, 16, 16, HEAD)
    return pl.pallas_call(
        gather_kernel,
        in_specs=[pl.BlockSpec(memory_space=vmem)],
        out_specs=pl.BlockSpec(memory_space=vmem),
        out_shape=jax.ShapeDtypeStruct(shape, BF16),
        scratch_shapes=[
            vmem(shape, BF16),
            vmem((2, 16, HEAD), BF16),
            vmem((2, 2, 16, HEAD), BF16),
            dma((1,)), dma((1,)), dma((1,)), dma((1,)),
            dma((4,)), dma((4,)), dma((4,)), dma((4,)),
        ],
        compiler_params=pltpu.CompilerParams(
            collective_id=0, has_side_effects=True, vmem_limit_bytes=40 << 20
        ),
    )(shard)


def attend_kernel(lengths, q, own, prompt, out, scores_a, scores_b, tops):
    length0, length1 = lengths[0], lengths[1]
    count0 = lax.div(length0 + TOKENS - 1, TOKENS)
    count1 = lax.div(length1 + TOKENS - 1, TOKENS)
    units = 2 * (count0 + count1)
    ones = jnp.ones((TILE, HEAD), BF16)

    def locate(unit):
        s = (unit >= 2 * count0).astype(jnp.int32)
        rest = unit - s * 2 * count0
        count = jnp.where(s == 0, count0, count1)
        g = (rest >= count).astype(jnp.int32)
        token = pl.multiple_of((rest - g * count) * TOKENS, TOKENS)
        return s, g, token, jnp.where(s == 0, length0, length1)

    def head_columns(g, head):
        return pl.ds(pl.multiple_of(g * HEADS * HEAD + head * HEAD, HEAD), HEAD)

    def step(current, scores_now, following, scores_next):
        if following is not None:
            s, g, token, length = locate(following)
            rows = pl.ds(token, TOKENS)
            queries = jnp.concatenate([q[s, rows, head_columns(g, h)] for h in range(HEADS)], 0)
            part_top = None
        if current is not None:
            s_now, g_now, token_now, length_now = locate(current)
            top = tops[...]
            top = jnp.concatenate([top, top], 1)
            total = jnp.zeros((ROWS, 2 * HEAD), F32)
        for k in range(5):
            keys = slice(k * TILE, (k + 1) * TILE)
            if following is not None:
                source = prompt[g, k, 0].reshape(TILE, HEAD) if k < 4 else own[s, g, 0]
                part = lax.dot_general(
                    queries, source, (((1,), (1,)), ((), ())), preferred_element_type=F32
                )
                if k == 4:
                    position = token + lax.rem(lax.broadcasted_iota(jnp.int32, (ROWS, TILE), 0), TOKENS)
                    key = lax.broadcasted_iota(jnp.int32, (ROWS, TILE), 1)
                    part = jnp.where((key <= position) & (key < length), part, NEG)
                scores_next[:, keys] = part
                part = jnp.maximum(part[:, :HEAD], part[:, HEAD:])
                part_top = part if part_top is None else jnp.maximum(part_top, part)
            if current is not None:
                weights = jnp.exp2((scores_now[:, keys] - top) * SCALE).astype(BF16)
                source = prompt[g_now, k, 1].reshape(TILE, HEAD) if k < 4 else own[s_now, g_now, 1]
                total += jnp.dot(
                    weights, jnp.concatenate([source, ones], 1), preferred_element_type=F32
                )
        if following is not None:
            tops[...] = jnp.broadcast_to(jnp.max(part_top, -1, keepdims=True), (ROWS, HEAD))
        if current is not None:
            result = total[:, :HEAD] / total[:, HEAD:]
            position = token_now + lax.rem(lax.broadcasted_iota(jnp.int32, (ROWS, HEAD), 0), TOKENS)
            result = jnp.where(position < length_now, result, 0.0).astype(BF16)
            for h in range(HEADS):
                out[s_now, pl.ds(token_now, TOKENS), head_columns(g_now, h)] = result[
                    h * TOKENS : (h + 1) * TOKENS
                ]

    step(None, None, 0, scores_a)

    @pl.loop(0, lax.div(units, 2))
    def _(pair):
        unit = 2 * pair
        step(unit, scores_a, unit + 1, scores_b)
        step(unit + 1, scores_b, jnp.minimum(unit + 2, units - 1), scores_a)

    for s, count in ((0, count0), (1, count1)):

        @pl.loop(count, SLOT // TOKENS)
        def _(i):
            out[s, pl.ds(pl.multiple_of(i * TOKENS, TOKENS), TOKENS), :] = jnp.zeros(
                (TOKENS, GROUPS * HEADS * HEAD), BF16
            )


def attend(lengths, queries, own, prompt):
    vmem = pltpu.VMEM
    return pl.pallas_call(
        attend_kernel,
        in_specs=[pl.BlockSpec(memory_space=pltpu.SMEM)] + [pl.BlockSpec(memory_space=vmem)] * 3,
        out_specs=pl.BlockSpec(memory_space=vmem),
        out_shape=jax.ShapeDtypeStruct(queries.shape, BF16),
        scratch_shapes=[
            vmem((ROWS, PROMPT + SLOT), F32),
            vmem((ROWS, PROMPT + SLOT), F32),
            vmem((ROWS, HEAD), F32),
        ],
        compiler_params=pltpu.CompilerParams(vmem_limit_bytes=50 << 20),
    )(lengths, queries, own, prompt)


def per_device(queries, trace_kv, lengths, prompt_kv):
    prompt = gather(prompt_kv)
    own = trace_kv[:, 0].reshape(2, SLOT, 2, GROUPS, HEAD).transpose(0, 3, 2, 1, 4)
    out = attend(lengths[:, 0], queries[:, 0], own, prompt)
    return out[:, None]


def solution(mesh):
    placed = (
        P(None, "dp", None, "tensor"),
        P(None, "dp", None, None, "tensor"),
        P(None, "dp"),
        P(("dp", "tensor"), None, None),
    )
    return jax.shard_map(
        per_device,
        mesh=mesh,
        in_specs=placed,
        out_specs=P(None, "dp", None, "tensor"),
        check_vma=False,
    )
```

```python
import math

import jax
import jax.numpy as jnp
from jax import lax
from jax.experimental import pallas as pl
from jax.experimental.pallas import tpu as pltpu
from jax.sharding import PartitionSpec as P

MESH = pl.DeviceIdType.MESH
BF16 = jnp.bfloat16
F32 = jnp.float32
HEAD = 128
HEADS = 8
GROUPS = 2
SLOT = 256
PROMPT = 1024
TILE = 256
TOKENS = 64
ROWS = TOKENS * HEADS
PAIRS = HEADS // 2
SCALE = math.log2(math.e) / math.sqrt(HEAD)
NEG = -1e30
PLANES = ((0, 1), (3, 2))


def turn(index, step):
    return lax.rem(index + step, 4)


def coordinates():
    dp, tensor = lax.axis_index("dp"), lax.axis_index("tensor")
    core = lax.rem(dp, 2)
    z = lax.rem(lax.div(dp, 2), 4)
    x = lax.rem(lax.div(dp, 8), 4)
    y = lax.div(dp, 32) * 2 + tensor
    return x, y, z, core


def device(x, y, z, core):
    return (((lax.div(y, 2) * 4 + x) * 4 + z) * 2 + core, lax.rem(y, 2))


def ring_hops(step):
    return min(step, 4 - step)


def remote(src, dst, send, recv, target):
    return pltpu.make_async_remote_copy(
        src_ref=src, dst_ref=dst, send_sem=send, recv_sem=recv, device_id=target, device_id_type=MESH
    )


def landed(ref, sem):
    pltpu.make_async_copy(ref, ref, sem).wait()


def head_columns(g, head):
    return pl.ds(pl.multiple_of(g * HEADS * HEAD + head * HEAD, HEAD), HEAD)


def first_kernel(
    lengths_hbm, shard_hbm, queries, trace_kv, out_hbm, kv_out, later_out,
    lengths, blocks, kv, shard, stage, q, raw, own, later, out, scores, tops,
    s1, r1, s3, r3, local,
):
    x, y, z, core = coordinates()
    tensor = lax.rem(y, 2)
    partner = device(x, y, z, 1 - core)
    away = [(a, b, c) for a in range(4) for b in range(4) for c in range(4) if a or b or c]
    away.sort(key=lambda step: -sum(map(ring_hops, step)))
    chips = [device(turn(x, a), turn(y, b), turn(z, c), core) for a, b, c in away]
    barrier = pltpu.get_barrier_semaphore()
    for peer in chips + [partner]:
        pl.semaphore_signal(barrier, inc=1, device_id=peer, device_id_type=MESH)
    load_shard = pltpu.make_async_copy(shard_hbm, shard, local.at[3])
    load_shard.start()
    load_lengths = pltpu.make_async_copy(lengths_hbm, lengths, local.at[6])
    load_lengths.start()
    load_q = pltpu.make_async_copy(queries.at[0], q, local.at[0])
    load_own = pltpu.make_async_copy(trace_kv, raw, local.at[1])
    load_q.start()
    load_own.start()
    load_shard.wait()
    for t in range(2):
        for k in range(2):
            columns = t * 2 * HEAD
            stage[t, k] = jnp.concatenate(
                [shard[:, k, columns : columns + HEAD], shard[:, k, columns + HEAD : columns + 2 * HEAD]], 0
            )
    here = x * 16 + y * 4 + z
    pl.semaphore_wait(barrier, len(chips) + 1)
    for k in range(2):
        for (_, b, _), target in zip(away, chips):
            to = lax.rem(turn(y, b), 2)
            remote(stage.at[to, k], blocks.at[core, k, here], s1.at[k], r1.at[k, x], target).start()
    for k in range(2):
        blocks[core, k, here] = stage[tensor, k]

    def scores_of(g, column, keys, mask=None):
        for j in range(PAIRS):
            pair = jnp.concatenate([q[:, head_columns(g, 2 * j)], q[:, head_columns(g, 2 * j + 1)]], 0)
            tile = lax.dot_general(pair, keys, (((1,), (1,)), ((), ())), preferred_element_type=F32)
            if mask is not None:
                tile = jnp.where(mask, tile, NEG)
            scores[g * PAIRS + j, :, column * TILE : (column + 1) * TILE] = tile
            tile = jnp.maximum(tile[:, :HEAD], tile[:, HEAD:])
            if mask is None:
                tile = jnp.maximum(tops[g * PAIRS + j], tile)
            tops[g * PAIRS + j] = tile

    load_own.wait()
    for s, target in ((0, own), (1, later)):
        for g in range(GROUPS):
            for k in range(2):
                target[g, k] = raw[s, :, k, g * HEAD : (g + 1) * HEAD]
    keep_later = pltpu.make_async_copy(later, later_out, local.at[4])
    keep_later.start()
    load_q.wait()
    load_lengths.wait()
    length = lengths[0]
    position = lax.rem(lax.broadcasted_iota(jnp.int32, (2 * SLOT, TILE), 0), SLOT)
    key = lax.broadcasted_iota(jnp.int32, (2 * SLOT, TILE), 1)
    allowed = (key <= position) & (key < length)

    @pl.loop(0, GROUPS)
    def _(g):
        scores_of(g, 4, own[g, 0], allowed)

    def group(side, k, d):
        return blocks.at[side, k, pl.ds(pl.multiple_of(turn(x, d) * 16, 16), 16)]

    def arrange(side, column, k):
        for g in range(GROUPS):
            rows = [group(side, k, d)[:, g * 8 : (g + 1) * 8].reshape(TILE // 2, HEAD) for d in PLANES[column % 2]]
            kv[g, column, k] = jnp.concatenate(rows, 0)

    def collect(k, column):
        for d in PLANES[column]:
            if d:
                landed(group(core, k, d), r1.at[k, turn(x, d)])
            else:
                landed(blocks.at[core, k, 0:15], r1.at[k, x])
            remote(group(core, k, d), group(core, k, d), s3.at[k, d], r3.at[k, d], partner).start()
        arrange(core, column, k)

    def collect_partner(k, column):
        for d in PLANES[column - 2]:
            landed(group(1 - core, k, d), r3.at[k, d])
        arrange(1 - core, column, k)

    def prompt_scores(column):
        @pl.loop(0, GROUPS)
        def _(g):
            scores_of(g, column, kv[g, column, 0])

    for column in (0, 1):
        collect(0, column)
    for column in (0, 1):
        prompt_scores(column)
    collect_partner(0, 2)
    prompt_scores(2)
    for column in (0, 1):
        collect(1, column)
    collect_partner(0, 3)
    prompt_scores(3)
    for pair in range(GROUPS * PAIRS):
        tops[pair] = jnp.broadcast_to(jnp.max(tops[pair], -1, keepdims=True), (2 * SLOT, HEAD))
    for column in (2, 3):
        collect_partner(1, column)
    keep = pltpu.make_async_copy(kv, kv_out, local.at[2])
    keep.start()

    ones = jnp.ones((TILE, HEAD), BF16)

    @pl.loop(0, GROUPS * PAIRS)
    def _(pair):
        g = lax.div(pair, PAIRS)
        top = jnp.concatenate([tops[pair], tops[pair]], 1)
        total = jnp.zeros((2 * SLOT, 2 * HEAD), F32)
        for column in range(5):
            tile = scores[pair, :, column * TILE : (column + 1) * TILE]
            weights = jnp.exp2((tile - top) * SCALE).astype(BF16)
            values = kv[g, column, 1] if column < 4 else own[g, 1]
            total += jnp.dot(weights, jnp.concatenate([values, ones], 1), preferred_element_type=F32)
        result = total[:, :HEAD] / total[:, HEAD:]
        result = jnp.where(position[:, :HEAD] < length, result, 0.0).astype(BF16)
        columns = pl.ds(pl.multiple_of(pair * 2 * HEAD, 2 * HEAD), 2 * HEAD)
        out[:, columns] = jnp.concatenate([result[:SLOT], result[SLOT:]], 1)
        pltpu.make_async_copy(out.at[:, columns], out_hbm.at[:, columns], local.at[5]).start()

    keep.wait()
    keep_later.wait()
    landed(out, local.at[5])
    for k in range(2):
        landed(blocks.at[core, k, 0:63], s1.at[k])
        for d in range(4):
            landed(group(core, k, d), s3.at[k, d])


def first(lengths, shard, queries, trace_kv):
    vmem, dma = pltpu.VMEM, pltpu.SemaphoreType.DMA
    gathered = (GROUPS, 4, 2, TILE, HEAD)
    columns = GROUPS * HEADS * HEAD
    own = (GROUPS, 2, SLOT, HEAD)
    return pl.pallas_call(
        first_kernel,
        in_specs=[pl.BlockSpec(memory_space=pltpu.HBM)] * 4,
        out_specs=[pl.BlockSpec(memory_space=pltpu.HBM)] * 3,
        out_shape=[
            jax.ShapeDtypeStruct((SLOT, columns), BF16),
            jax.ShapeDtypeStruct(gathered, BF16),
            jax.ShapeDtypeStruct(own, BF16),
        ],
        scratch_shapes=[
            pltpu.SMEM((2,), jnp.int32),
            vmem((2, 2, 64, 16, HEAD), BF16),
            vmem(gathered, BF16),
            vmem((8, 2, 2 * GROUPS * HEAD), BF16),
            vmem((2, 2, 16, HEAD), BF16),
            vmem((SLOT, columns), BF16),
            vmem((2, SLOT, 2, GROUPS * HEAD), BF16),
            vmem(own, BF16),
            vmem(own, BF16),
            vmem((SLOT, columns), BF16),
            vmem((2 * PAIRS, 2 * SLOT, PROMPT + SLOT), F32),
            vmem((2 * PAIRS, 2 * SLOT, HEAD), F32),
            dma((2,)), dma((2, 4)), dma((2, 4)), dma((2, 4)), dma((7,)),
        ],
        compiler_params=pltpu.CompilerParams(
            collective_id=0, has_side_effects=True, vmem_limit_bytes=44 << 20
        ),
    )(lengths, shard, queries, trace_kv)


def second_kernel(lengths, q, own, prompt, done, out, scores_a, scores_b, tops, result_ref, local):
    carry_over = pltpu.make_async_copy(done, out.at[0], local.at[0])
    carry_over.start()
    length = lengths[1]
    count = lax.div(length + TOKENS - 1, TOKENS)
    units = 2 * count
    ones = jnp.ones((TILE, HEAD), BF16)

    def locate(unit):
        g = (unit >= count).astype(jnp.int32)
        return g, pl.multiple_of((unit - g * count) * TOKENS, TOKENS)

    def step(current, scores_now, following, scores_next):
        if following is not None:
            g, token = locate(following)
            rows = pl.ds(token, TOKENS)
            queries = jnp.concatenate([q[1, rows, head_columns(g, h)] for h in range(HEADS)], 0)
            part_top = None
        if current is not None:
            g_now, token_now = locate(current)
            top = tops[...]
            top = jnp.concatenate([top, top], 1)
            total = jnp.zeros((ROWS, 2 * HEAD), F32)
        for k in range(5):
            keys = slice(k * TILE, (k + 1) * TILE)
            if following is not None:
                source = prompt[g, k, 0] if k < 4 else own[g, 0]
                part = lax.dot_general(
                    queries, source, (((1,), (1,)), ((), ())), preferred_element_type=F32
                )
                if k == 4:
                    position = token + lax.rem(lax.broadcasted_iota(jnp.int32, (ROWS, TILE), 0), TOKENS)
                    key = lax.broadcasted_iota(jnp.int32, (ROWS, TILE), 1)
                    part = jnp.where((key <= position) & (key < length), part, NEG)
                scores_next[:, keys] = part
                part = jnp.maximum(part[:, :HEAD], part[:, HEAD:])
                part_top = part if part_top is None else jnp.maximum(part_top, part)
            if current is not None:
                weights = jnp.exp2((scores_now[:, keys] - top) * SCALE).astype(BF16)
                source = prompt[g_now, k, 1] if k < 4 else own[g_now, 1]
                total += jnp.dot(
                    weights, jnp.concatenate([source, ones], 1), preferred_element_type=F32
                )
        if following is not None:
            tops[...] = jnp.broadcast_to(jnp.max(part_top, -1, keepdims=True), (ROWS, HEAD))
        if current is not None:
            result = total[:, :HEAD] / total[:, HEAD:]
            position = token_now + lax.rem(lax.broadcasted_iota(jnp.int32, (ROWS, HEAD), 0), TOKENS)
            result = jnp.where(position < length, result, 0.0).astype(BF16)
            for h in range(HEADS):
                result_ref[pl.ds(token_now, TOKENS), head_columns(g_now, h)] = result[
                    h * TOKENS : (h + 1) * TOKENS
                ]

    @pl.loop(count, SLOT // TOKENS)
    def _(i):
        result_ref[pl.ds(pl.multiple_of(i * TOKENS, TOKENS), TOKENS), :] = jnp.zeros(
            (TOKENS, GROUPS * HEADS * HEAD), BF16
        )

    step(None, None, 0, scores_a)

    @pl.loop(0, count)
    def _(pair):
        unit = 2 * pair
        step(unit, scores_a, unit + 1, scores_b)
        step(unit + 1, scores_b, jnp.minimum(unit + 2, units - 1), scores_a)

    store = pltpu.make_async_copy(result_ref, out.at[1], local.at[1])
    store.start()
    carry_over.wait()
    store.wait()


def second(lengths, queries, own, prompt, done):
    vmem = pltpu.VMEM
    return pl.pallas_call(
        second_kernel,
        in_specs=[pl.BlockSpec(memory_space=pltpu.SMEM)] + [pl.BlockSpec(memory_space=vmem)] * 4,
        out_specs=pl.BlockSpec(memory_space=pltpu.HBM),
        out_shape=jax.ShapeDtypeStruct(queries.shape, BF16),
        scratch_shapes=[
            vmem((ROWS, PROMPT + SLOT), F32),
            vmem((ROWS, PROMPT + SLOT), F32),
            vmem((ROWS, HEAD), F32),
            vmem((SLOT, GROUPS * HEADS * HEAD), BF16),
            pltpu.SemaphoreType.DMA((2,)),
        ],
        compiler_params=pltpu.CompilerParams(vmem_limit_bytes=40 << 20),
    )(lengths, queries, own, prompt, done)


def per_device(queries, trace_kv, lengths, prompt_kv):
    lengths, queries = lengths[:, 0], queries[:, 0]
    arguments = (lengths, prompt_kv, queries, trace_kv[:, 0])
    done, prompt, own = first(*(pltpu.with_memory_space_constraint(a, pltpu.HBM) for a in arguments))
    return second(lengths, queries, own, prompt, done)[:, None]


def solution(mesh):
    placed = (
        P(None, "dp", None, "tensor"),
        P(None, "dp", None, None, "tensor"),
        P(None, "dp"),
        P(("dp", "tensor"), None, None),
    )
    return jax.shard_map(
        per_device,
        mesh=mesh,
        in_specs=placed,
        out_specs=P(None, "dp", None, "tensor"),
        check_vma=False,
    )
```

```python
import math

import jax
import jax.numpy as jnp
from jax import lax
from jax.experimental import pallas as pl
from jax.experimental.pallas import tpu as pltpu
from jax.sharding import PartitionSpec as P

MESH = pl.DeviceIdType.MESH
BF16 = jnp.bfloat16
F32 = jnp.float32
HEAD = 128
HEADS = 8
GROUPS = 2
SLOT = 256
PROMPT = 1024
TILE = 256
TOKENS = 64
ROWS = TOKENS * HEADS
PAIRS = HEADS // 2
SCALE = math.log2(math.e) / math.sqrt(HEAD)
NEG = -1e30
PLANES = ((0, 1), (3, 2))


def turn(index, step):
    return lax.rem(index + step, 4)


def coordinates():
    dp, tensor = lax.axis_index("dp"), lax.axis_index("tensor")
    core = lax.rem(dp, 2)
    z = lax.rem(lax.div(dp, 2), 4)
    x = lax.rem(lax.div(dp, 8), 4)
    y = lax.div(dp, 32) * 2 + tensor
    return x, y, z, core


def device(x, y, z, core):
    return (((lax.div(y, 2) * 4 + x) * 4 + z) * 2 + core, lax.rem(y, 2))


def ring_hops(step):
    return min(step, 4 - step)


def remote(src, dst, send, recv, target):
    return pltpu.make_async_remote_copy(
        src_ref=src, dst_ref=dst, send_sem=send, recv_sem=recv, device_id=target, device_id_type=MESH
    )


def landed(ref, sem):
    pltpu.make_async_copy(ref, ref, sem).wait()


def head_columns(g, head):
    return pl.ds(pl.multiple_of(g * HEADS * HEAD + head * HEAD, HEAD), HEAD)


def first_kernel(
    lengths_hbm, shard_hbm, queries, trace_kv, out_hbm, kv_out, later_out,
    lengths, blocks, kv, shard, stage, q, raw, own, later, out, scores, tops,
    s1, r1, s3, r3, local,
):
    x, y, z, core = coordinates()
    tensor = lax.rem(y, 2)
    partner = device(x, y, z, 1 - core)
    load_shard = pltpu.make_async_copy(shard_hbm, shard, local.at[3])
    load_shard.start()
    away = [(a, b, c) for a in range(4) for b in range(4) for c in range(4) if a or b or c]
    away.sort(key=lambda step: -sum(map(ring_hops, step)))
    rows = [turn(y, b) for b in range(4)]
    row_tensor = [lax.rem(row, 2) for row in rows]
    row_base = [lax.div(row, 2) * 32 for row in rows]
    column_base = [[turn(x, a) * 8 + turn(z, c) * 2 + core for c in range(4)] for a in range(4)]

    def chip(step):
        a, b, c = step
        return row_base[b] + column_base[a][c], row_tensor[b]

    barrier = pltpu.get_barrier_semaphore()
    for step in away:
        pl.semaphore_signal(barrier, inc=1, device_id=chip(step), device_id_type=MESH)
    pl.semaphore_signal(barrier, inc=1, device_id=partner, device_id_type=MESH)
    load_lengths = pltpu.make_async_copy(lengths_hbm, lengths, local.at[6])
    load_lengths.start()
    load_q = pltpu.make_async_copy(queries.at[0], q, local.at[0])
    load_own = pltpu.make_async_copy(trace_kv, raw, local.at[1])
    load_q.start()
    load_own.start()
    load_shard.wait()
    for t in range(2):
        for k in range(2):
            columns = t * 2 * HEAD
            stage[t, k] = jnp.concatenate(
                [shard[:, k, columns : columns + HEAD], shard[:, k, columns + HEAD : columns + 2 * HEAD]], 0
            )
    here = x * 16 + y * 4 + z
    pl.semaphore_wait(barrier, len(away) + 1)
    for k in range(2):
        for step in away:
            block = stage.at[row_tensor[step[1]], k]
            remote(block, blocks.at[core, k, here], s1.at[k], r1.at[k, x], chip(step)).start()
    for k in range(2):
        blocks[core, k, here] = stage[tensor, k]

    def scores_of(g, column, keys, mask=None):
        for j in range(PAIRS):
            pair = jnp.concatenate([q[:, head_columns(g, 2 * j)], q[:, head_columns(g, 2 * j + 1)]], 0)
            tile = lax.dot_general(pair, keys, (((1,), (1,)), ((), ())), preferred_element_type=F32)
            if mask is not None:
                tile = jnp.where(mask, tile, NEG)
            scores[g * PAIRS + j, :, column * TILE : (column + 1) * TILE] = tile
            tile = jnp.maximum(tile[:, :HEAD], tile[:, HEAD:])
            if mask is None:
                tile = jnp.maximum(tops[g * PAIRS + j], tile)
            tops[g * PAIRS + j] = tile

    load_own.wait()
    for s, target in ((0, own), (1, later)):
        for g in range(GROUPS):
            for k in range(2):
                target[g, k] = raw[s, :, k, g * HEAD : (g + 1) * HEAD]
    keep_later = pltpu.make_async_copy(later, later_out, local.at[4])
    keep_later.start()
    load_q.wait()
    load_lengths.wait()
    length = lengths[0]
    position = lax.rem(lax.broadcasted_iota(jnp.int32, (2 * SLOT, TILE), 0), SLOT)
    key = lax.broadcasted_iota(jnp.int32, (2 * SLOT, TILE), 1)
    allowed = (key <= position) & (key < length)

    @pl.loop(0, GROUPS)
    def _(g):
        scores_of(g, 4, own[g, 0], allowed)

    def group(side, k, d):
        return blocks.at[side, k, pl.ds(pl.multiple_of(turn(x, d) * 16, 16), 16)]

    def arrange(side, column, k):
        for g in range(GROUPS):
            rows = [group(side, k, d)[:, g * 8 : (g + 1) * 8].reshape(TILE // 2, HEAD) for d in PLANES[column % 2]]
            kv[g, column, k] = jnp.concatenate(rows, 0)

    def collect(k, column):
        for d in PLANES[column]:
            if d:
                landed(group(core, k, d), r1.at[k, turn(x, d)])
            else:
                landed(blocks.at[core, k, 0:15], r1.at[k, x])
            remote(group(core, k, d), group(core, k, d), s3.at[k, d], r3.at[k, d], partner).start()
        arrange(core, column, k)

    def collect_partner(k, column):
        for d in PLANES[column - 2]:
            landed(group(1 - core, k, d), r3.at[k, d])
        arrange(1 - core, column, k)

    def prompt_scores(column):
        @pl.loop(0, GROUPS)
        def _(g):
            scores_of(g, column, kv[g, column, 0])

    for column in (0, 1):
        collect(0, column)
    for column in (0, 1):
        prompt_scores(column)
    collect_partner(0, 2)
    prompt_scores(2)
    for column in (0, 1):
        collect(1, column)
    collect_partner(0, 3)
    for g in range(GROUPS):
        scores_of(g, 3, kv[g, 3, 0])
        for pair in range(g * PAIRS, (g + 1) * PAIRS):
            tops[pair] = jnp.broadcast_to(jnp.max(tops[pair], -1, keepdims=True), (2 * SLOT, HEAD))
    for column in (2, 3):
        collect_partner(1, column)
    keep = pltpu.make_async_copy(kv, kv_out, local.at[2])
    keep.start()

    ones = jnp.ones((TILE, HEAD), BF16)

    @pl.loop(0, GROUPS * PAIRS // 2)
    def _(step):
        pairs = [2 * step, 2 * step + 1]
        g = lax.div(step, PAIRS // 2)
        totals = [jnp.zeros((2 * SLOT, 2 * HEAD), F32) for _ in pairs]
        for column in range(5):
            values = kv[g, column, 1] if column < 4 else own[g, 1]
            values = jnp.concatenate([values, ones], 1)
            for i, pair in enumerate(pairs):
                top = jnp.concatenate([tops[pair], tops[pair]], 1)
                tile = scores[pair, :, column * TILE : (column + 1) * TILE]
                weights = jnp.exp2((tile - top) * SCALE).astype(BF16)
                totals[i] += jnp.dot(weights, values, preferred_element_type=F32)
        for pair, total in zip(pairs, totals):
            result = total[:, :HEAD] / total[:, HEAD:]
            result = jnp.where(position[:, :HEAD] < length, result, 0.0).astype(BF16)
            columns = pl.ds(pl.multiple_of(pair * 2 * HEAD, 2 * HEAD), 2 * HEAD)
            out[:, columns] = jnp.concatenate([result[:SLOT], result[SLOT:]], 1)
            pltpu.make_async_copy(out.at[:, columns], out_hbm.at[:, columns], local.at[5]).start()

    keep.wait()
    keep_later.wait()
    landed(out, local.at[5])
    for k in range(2):
        landed(blocks.at[core, k, 0:63], s1.at[k])
        for d in range(4):
            landed(group(core, k, d), s3.at[k, d])


def first(lengths, shard, queries, trace_kv):
    vmem, dma = pltpu.VMEM, pltpu.SemaphoreType.DMA
    gathered = (GROUPS, 4, 2, TILE, HEAD)
    columns = GROUPS * HEADS * HEAD
    own = (GROUPS, 2, SLOT, HEAD)
    return pl.pallas_call(
        first_kernel,
        in_specs=[pl.BlockSpec(memory_space=pltpu.HBM)] * 4,
        out_specs=[pl.BlockSpec(memory_space=pltpu.HBM)] * 3,
        out_shape=[
            jax.ShapeDtypeStruct((SLOT, columns), BF16),
            jax.ShapeDtypeStruct(gathered, BF16),
            jax.ShapeDtypeStruct(own, BF16),
        ],
        scratch_shapes=[
            pltpu.SMEM((2,), jnp.int32),
            vmem((2, 2, 64, 16, HEAD), BF16),
            vmem(gathered, BF16),
            vmem((8, 2, 2 * GROUPS * HEAD), BF16),
            vmem((2, 2, 16, HEAD), BF16),
            vmem((SLOT, columns), BF16),
            vmem((2, SLOT, 2, GROUPS * HEAD), BF16),
            vmem(own, BF16),
            vmem(own, BF16),
            vmem((SLOT, columns), BF16),
            vmem((2 * PAIRS, 2 * SLOT, PROMPT + SLOT), F32),
            vmem((2 * PAIRS, 2 * SLOT, HEAD), F32),
            dma((2,)), dma((2, 4)), dma((2, 4)), dma((2, 4)), dma((7,)),
        ],
        compiler_params=pltpu.CompilerParams(
            collective_id=0, has_side_effects=True, vmem_limit_bytes=44 << 20
        ),
    )(lengths, shard, queries, trace_kv)


def second_kernel(lengths, q, own, prompt, done, out, scores_a, scores_b, tops, result_ref, local):
    carry_over = pltpu.make_async_copy(done, out.at[0], local.at[0])
    carry_over.start()
    length = lengths[1]
    full = lax.div(length + TOKENS // 2 - 1, TOKENS)
    half = full * TOKENS < length
    ones = jnp.ones((TILE, HEAD), BF16)

    def store(token, tokens):
        rows = pl.ds(pl.multiple_of(token, tokens), tokens)
        pltpu.make_async_copy(result_ref.at[rows], out.at[1, rows], local.at[1]).start()

    def step(tokens, current, scores_now, following, scores_next):
        rows = tokens * HEADS
        position = lax.rem(lax.broadcasted_iota(jnp.int32, (rows, TILE), 0), tokens)
        if following is not None:
            g, token = following
            token = pl.multiple_of(token, tokens)
            queries = jnp.concatenate(
                [q[1, pl.ds(token, tokens), head_columns(g, h)] for h in range(HEADS)], 0
            )
            part_top = None
        if current is not None:
            g_now, token_now = current
            token_now = pl.multiple_of(token_now, tokens)
            top = tops[:rows]
            top = jnp.concatenate([top, top], 1)
            total = jnp.zeros((rows, 2 * HEAD), F32)
        for k in range(5):
            keys = slice(k * TILE, (k + 1) * TILE)
            if following is not None:
                source = prompt[g, k, 0] if k < 4 else own[g, 0]
                part = lax.dot_general(
                    queries, source, (((1,), (1,)), ((), ())), preferred_element_type=F32
                )
                if k == 4:
                    key = lax.broadcasted_iota(jnp.int32, (rows, TILE), 1)
                    part = jnp.where((key <= position + token) & (key < length), part, NEG)
                scores_next[:rows, keys] = part
                part = jnp.maximum(part[:, :HEAD], part[:, HEAD:])
                part_top = part if part_top is None else jnp.maximum(part_top, part)
            if current is not None:
                weights = jnp.exp2((scores_now[:rows, keys] - top) * SCALE).astype(BF16)
                source = prompt[g_now, k, 1] if k < 4 else own[g_now, 1]
                total += jnp.dot(
                    weights, jnp.concatenate([source, ones], 1), preferred_element_type=F32
                )
        if following is not None:
            tops[:rows] = jnp.broadcast_to(jnp.max(part_top, -1, keepdims=True), (rows, HEAD))
        if current is not None:
            result = total[:, :HEAD] / total[:, HEAD:]
            result = jnp.where(position[:, :HEAD] + token_now < length, result, 0.0).astype(BF16)
            for h in range(HEADS):
                result_ref[pl.ds(token_now, tokens), head_columns(g_now, h)] = result[
                    h * tokens : (h + 1) * tokens
                ]

    covered = full + half.astype(jnp.int32)

    @pl.loop(covered, SLOT // TOKENS)
    def _(i):
        token = pl.multiple_of(i * TOKENS, TOKENS)
        result_ref[pl.ds(token, TOKENS), :] = jnp.zeros((TOKENS, GROUPS * HEADS * HEAD), BF16)
        store(token, TOKENS)

    @pl.when(full > 0)
    def _():
        step(TOKENS, None, None, (0, 0), scores_a)

        @pl.loop(0, full - 1)
        def _(i):
            token = i * TOKENS
            step(TOKENS, (0, token), scores_a, (1, token), scores_b)
            step(TOKENS, (1, token), scores_b, (0, token + TOKENS), scores_a)
            store(token, TOKENS)

        token = (full - 1) * TOKENS
        step(TOKENS, (0, token), scores_a, (1, token), scores_b)
        step(TOKENS, (1, token), scores_b, None, None)
        store(token, TOKENS)

    @pl.when(half)
    def _():
        tokens = TOKENS // 2
        token = full * TOKENS
        step(tokens, None, None, (0, token), scores_a)
        step(tokens, (0, token), scores_a, (1, token), scores_b)
        step(tokens, (1, token), scores_b, None, None)
        rest = pl.ds(pl.multiple_of(token + tokens, tokens), tokens)
        result_ref[rest, :] = jnp.zeros((tokens, GROUPS * HEADS * HEAD), BF16)
        store(token, TOKENS)

    pltpu.make_async_copy(result_ref, out.at[1], local.at[1]).wait()
    carry_over.wait()


def second(lengths, queries, own, prompt, done):
    vmem = pltpu.VMEM
    return pl.pallas_call(
        second_kernel,
        in_specs=[pl.BlockSpec(memory_space=pltpu.SMEM)] + [pl.BlockSpec(memory_space=vmem)] * 4,
        out_specs=pl.BlockSpec(memory_space=pltpu.HBM),
        out_shape=jax.ShapeDtypeStruct(queries.shape, BF16),
        scratch_shapes=[
            vmem((ROWS, PROMPT + SLOT), F32),
            vmem((ROWS, PROMPT + SLOT), F32),
            vmem((ROWS, HEAD), F32),
            vmem((SLOT, GROUPS * HEADS * HEAD), BF16),
            pltpu.SemaphoreType.DMA((2,)),
        ],
        compiler_params=pltpu.CompilerParams(vmem_limit_bytes=40 << 20),
    )(lengths, queries, own, prompt, done)


def per_device(queries, trace_kv, lengths, prompt_kv):
    lengths, queries = lengths[:, 0], queries[:, 0]
    arguments = (lengths, prompt_kv, queries, trace_kv[:, 0])
    done, prompt, own = first(*(pltpu.with_memory_space_constraint(a, pltpu.HBM) for a in arguments))
    return second(lengths, queries, own, prompt, done)[:, None]


def solution(mesh):
    placed = (
        P(None, "dp", None, "tensor"),
        P(None, "dp", None, None, "tensor"),
        P(None, "dp"),
        P(("dp", "tensor"), None, None),
    )
    return jax.shard_map(
        per_device,
        mesh=mesh,
        in_specs=placed,
        out_specs=P(None, "dp", None, "tensor"),
        check_vma=False,
    )
```

```python
import math

import jax
import jax.numpy as jnp
from jax import lax
from jax.experimental import pallas as pl
from jax.experimental.pallas import tpu as pltpu
from jax.sharding import PartitionSpec as P

MESH = pl.DeviceIdType.MESH
BF16 = jnp.bfloat16
F32 = jnp.float32
HEAD = 128
HEADS = 8
GROUPS = 2
SLOT = 256
PROMPT = 1024
TILE = 256
TOKENS = 64
ROWS = TOKENS * HEADS
PAIRS = HEADS // 2
SCALE = math.log2(math.e) / math.sqrt(HEAD)
NEG = -1e30
PLANES = ((0, 1), (3, 2))


def turn(index, step):
    return lax.rem(index + step, 4)


def coordinates():
    dp, tensor = lax.axis_index("dp"), lax.axis_index("tensor")
    core = lax.rem(dp, 2)
    z = lax.rem(lax.div(dp, 2), 4)
    x = lax.rem(lax.div(dp, 8), 4)
    y = lax.div(dp, 32) * 2 + tensor
    return x, y, z, core


def device(x, y, z, core):
    return (((lax.div(y, 2) * 4 + x) * 4 + z) * 2 + core, lax.rem(y, 2))


def ring_hops(step):
    return min(step, 4 - step)


def remote(src, dst, send, recv, target):
    return pltpu.make_async_remote_copy(
        src_ref=src, dst_ref=dst, send_sem=send, recv_sem=recv, device_id=target, device_id_type=MESH
    )


def landed(ref, sem):
    pltpu.make_async_copy(ref, ref, sem).wait()


def head_columns(g, head):
    return pl.ds(pl.multiple_of(g * HEADS * HEAD + head * HEAD, HEAD), HEAD)


def first_kernel(
    lengths_hbm, shard_hbm, queries, trace_kv, out_hbm, kv_out, later_out,
    lengths, blocks, kv, shard, stage, q, raw, own, later, out, scores, tops, partial,
    s1, r1, s3, r3, local,
):
    x, y, z, core = coordinates()
    tensor = lax.rem(y, 2)
    partner = device(x, y, z, 1 - core)
    load_shard = pltpu.make_async_copy(shard_hbm, shard, local.at[3])
    load_shard.start()
    away = [(a, b, c) for a in range(4) for b in range(4) for c in range(4) if a or b or c]
    away.sort(key=lambda step: -sum(map(ring_hops, step)))
    rows = [turn(y, b) for b in range(4)]
    row_tensor = [lax.rem(row, 2) for row in rows]
    row_base = [lax.div(row, 2) * 32 for row in rows]
    column_base = [[turn(x, a) * 8 + turn(z, c) * 2 + core for c in range(4)] for a in range(4)]

    def chip(step):
        a, b, c = step
        return row_base[b] + column_base[a][c], row_tensor[b]

    barrier = pltpu.get_barrier_semaphore()
    for step in away:
        pl.semaphore_signal(barrier, inc=1, device_id=chip(step), device_id_type=MESH)
    pl.semaphore_signal(barrier, inc=1, device_id=partner, device_id_type=MESH)
    load_lengths = pltpu.make_async_copy(lengths_hbm, lengths, local.at[6])
    load_lengths.start()
    load_q = pltpu.make_async_copy(queries.at[0], q, local.at[0])
    load_own = pltpu.make_async_copy(trace_kv, raw, local.at[1])
    load_q.start()
    load_own.start()
    load_shard.wait()
    for t in range(2):
        for k in range(2):
            columns = t * 2 * HEAD
            stage[t, k] = jnp.concatenate(
                [shard[:, k, columns : columns + HEAD], shard[:, k, columns + HEAD : columns + 2 * HEAD]], 0
            )
    here = x * 16 + y * 4 + z
    pl.semaphore_wait(barrier, len(away) + 1)
    for k in range(2):
        for step in away:
            block = stage.at[row_tensor[step[1]], k]
            remote(block, blocks.at[core, k, here], s1.at[k], r1.at[k, x], chip(step)).start()
    for k in range(2):
        blocks[core, k, here] = stage[tensor, k]

    def scores_of(g, columns, mask=None):
        for j in range(PAIRS):
            pair = jnp.concatenate([q[:, head_columns(g, 2 * j)], q[:, head_columns(g, 2 * j + 1)]], 0)
            top = None if mask is not None else tops[g * PAIRS + j]
            for column in columns:
                keys = kv[g, column, 0] if column < 4 else own[g, 0]
                tile = lax.dot_general(pair, keys, (((1,), (1,)), ((), ())), preferred_element_type=F32)
                if mask is not None:
                    tile = jnp.where(mask, tile, NEG)
                scores[g * PAIRS + j, :, column * TILE : (column + 1) * TILE] = tile
                tile = jnp.maximum(tile[:, :HEAD], tile[:, HEAD:])
                top = tile if top is None else jnp.maximum(top, tile)
            tops[g * PAIRS + j] = top

    load_own.wait()
    for s, target in ((0, own), (1, later)):
        for g in range(GROUPS):
            for k in range(2):
                target[g, k] = raw[s, :, k, g * HEAD : (g + 1) * HEAD]
    keep_later = pltpu.make_async_copy(later, later_out, local.at[4])
    keep_later.start()
    load_q.wait()
    load_lengths.wait()
    length = lengths[0]
    position = lax.rem(lax.broadcasted_iota(jnp.int32, (2 * SLOT, TILE), 0), SLOT)
    key = lax.broadcasted_iota(jnp.int32, (2 * SLOT, TILE), 1)
    allowed = (key <= position) & (key < length)

    @pl.loop(0, GROUPS)
    def _(g):
        scores_of(g, (4,), allowed)

    def group(side, k, d):
        return blocks.at[side, k, pl.ds(pl.multiple_of(turn(x, d) * 16, 16), 16)]

    def arrange(side, column, k):
        for g in range(GROUPS):
            rows = [group(side, k, d)[:, g * 8 : (g + 1) * 8].reshape(TILE // 2, HEAD) for d in PLANES[column % 2]]
            kv[g, column, k] = jnp.concatenate(rows, 0)

    def collect(k, column):
        for d in PLANES[column]:
            if d:
                landed(group(core, k, d), r1.at[k, turn(x, d)])
            else:
                landed(blocks.at[core, k, 0:15], r1.at[k, x])
            remote(group(core, k, d), group(core, k, d), s3.at[k, d], r3.at[k, d], partner).start()
        arrange(core, column, k)

    def collect_partner(k, column):
        for d in PLANES[column - 2]:
            landed(group(1 - core, k, d), r3.at[k, d])
        arrange(1 - core, column, k)

    for column in (0, 1):
        collect(0, column)

    @pl.loop(0, GROUPS)
    def _(g):
        scores_of(g, (0, 1))

    for column in (2, 3):
        collect_partner(0, column)
    for g in range(GROUPS):
        scores_of(g, (2, 3))
        for pair in range(g * PAIRS, (g + 1) * PAIRS):
            tops[pair] = jnp.broadcast_to(jnp.max(tops[pair], -1, keepdims=True), (2 * SLOT, HEAD))
        if g == 0:
            collect(1, 0)
            collect(1, 1)
    ones = jnp.ones((TILE, HEAD), BF16)

    def attended(step, columns):
        g = lax.div(step, PAIRS // 2)
        totals = [None, None]
        for column in columns:
            values = kv[g, column, 1] if column < 4 else own[g, 1]
            values = jnp.concatenate([values, ones], 1)
            for i in range(2):
                pair = 2 * step + i
                top = jnp.concatenate([tops[pair], tops[pair]], 1)
                tile = scores[pair, :, column * TILE : (column + 1) * TILE]
                weights = jnp.exp2((tile - top) * SCALE).astype(BF16)
                total = jnp.dot(weights, values, preferred_element_type=F32)
                totals[i] = total if totals[i] is None else totals[i] + total
        return totals

    def finish(step, totals):
        for i, total in enumerate(totals):
            pair = 2 * step + i
            result = total[:, :HEAD] / total[:, HEAD:]
            result = jnp.where(position[:, :HEAD] < length, result, 0.0).astype(BF16)
            columns = pl.ds(pl.multiple_of(pair * 2 * HEAD, 2 * HEAD), 2 * HEAD)
            out[:, columns] = jnp.concatenate([result[:SLOT], result[SLOT:]], 1)
            pltpu.make_async_copy(out.at[:, columns], out_hbm.at[:, columns], local.at[5]).start()

    for i, total in enumerate(attended(0, (4, 0, 1))):
        partial[i] = total
    for column in (2, 3):
        collect_partner(1, column)
    keep = pltpu.make_async_copy(kv, kv_out, local.at[2])
    keep.start()
    finish(0, [partial[i] + total for i, total in enumerate(attended(0, (2, 3)))])

    @pl.loop(1, PAIRS)
    def _(step):
        finish(step, attended(step, (0, 1, 2, 3, 4)))

    keep.wait()
    keep_later.wait()
    landed(out, local.at[5])
    for k in range(2):
        landed(blocks.at[core, k, 0:63], s1.at[k])
        for d in range(4):
            landed(group(core, k, d), s3.at[k, d])


def first(lengths, shard, queries, trace_kv):
    vmem, dma = pltpu.VMEM, pltpu.SemaphoreType.DMA
    gathered = (GROUPS, 4, 2, TILE, HEAD)
    columns = GROUPS * HEADS * HEAD
    own = (GROUPS, 2, SLOT, HEAD)
    return pl.pallas_call(
        first_kernel,
        in_specs=[pl.BlockSpec(memory_space=pltpu.HBM)] * 4,
        out_specs=[pl.BlockSpec(memory_space=pltpu.HBM)] * 3,
        out_shape=[
            jax.ShapeDtypeStruct((SLOT, columns), BF16),
            jax.ShapeDtypeStruct(gathered, BF16),
            jax.ShapeDtypeStruct(own, BF16),
        ],
        scratch_shapes=[
            pltpu.SMEM((2,), jnp.int32),
            vmem((2, 2, 64, 16, HEAD), BF16),
            vmem(gathered, BF16),
            vmem((8, 2, 2 * GROUPS * HEAD), BF16),
            vmem((2, 2, 16, HEAD), BF16),
            vmem((SLOT, columns), BF16),
            vmem((2, SLOT, 2, GROUPS * HEAD), BF16),
            vmem(own, BF16),
            vmem(own, BF16),
            vmem((SLOT, columns), BF16),
            vmem((2 * PAIRS, 2 * SLOT, PROMPT + SLOT), F32),
            vmem((2 * PAIRS, 2 * SLOT, HEAD), F32),
            vmem((2, 2 * SLOT, 2 * HEAD), F32),
            dma((2,)), dma((2, 4)), dma((2, 4)), dma((2, 4)), dma((7,)),
        ],
        compiler_params=pltpu.CompilerParams(
            collective_id=0, has_side_effects=True, vmem_limit_bytes=44 << 20
        ),
    )(lengths, shard, queries, trace_kv)


def second_kernel(lengths, q, own, prompt, done, out, scores_a, scores_b, tops, result_ref, local):
    carry_over = pltpu.make_async_copy(done, out.at[0], local.at[0])
    carry_over.start()
    length = lengths[1]
    full = lax.div(length + TOKENS // 2 - 1, TOKENS)
    half = full * TOKENS < length
    ones = jnp.ones((TILE, HEAD), BF16)

    def store(token, tokens):
        rows = pl.ds(pl.multiple_of(token, tokens), tokens)
        pltpu.make_async_copy(result_ref.at[rows], out.at[1, rows], local.at[1]).start()

    def step(tokens, current, scores_now, following, scores_next):
        rows = tokens * HEADS
        position = lax.rem(lax.broadcasted_iota(jnp.int32, (rows, TILE), 0), tokens)
        if following is not None:
            g, token = following
            token = pl.multiple_of(token, tokens)
            queries = jnp.concatenate(
                [q[1, pl.ds(token, tokens), head_columns(g, h)] for h in range(HEADS)], 0
            )
            part_top = None
        if current is not None:
            g_now, token_now = current
            token_now = pl.multiple_of(token_now, tokens)
            top = tops[:rows]
            top = jnp.concatenate([top, top], 1)
            total = jnp.zeros((rows, 2 * HEAD), F32)
        for k in range(5):
            keys = slice(k * TILE, (k + 1) * TILE)
            if following is not None:
                source = prompt[g, k, 0] if k < 4 else own[g, 0]
                part = lax.dot_general(
                    queries, source, (((1,), (1,)), ((), ())), preferred_element_type=F32
                )
                if k == 4:
                    key = lax.broadcasted_iota(jnp.int32, (rows, TILE), 1)
                    part = jnp.where((key <= position + token) & (key < length), part, NEG)
                scores_next[:rows, keys] = part
                part = jnp.maximum(part[:, :HEAD], part[:, HEAD:])
                part_top = part if part_top is None else jnp.maximum(part_top, part)
            if current is not None:
                weights = jnp.exp2((scores_now[:rows, keys] - top) * SCALE).astype(BF16)
                source = prompt[g_now, k, 1] if k < 4 else own[g_now, 1]
                total += jnp.dot(
                    weights, jnp.concatenate([source, ones], 1), preferred_element_type=F32
                )
        if following is not None:
            tops[:rows] = jnp.broadcast_to(jnp.max(part_top, -1, keepdims=True), (rows, HEAD))
        if current is not None:
            result = total[:, :HEAD] / total[:, HEAD:]
            result = jnp.where(position[:, :HEAD] + token_now < length, result, 0.0).astype(BF16)
            for h in range(HEADS):
                result_ref[pl.ds(token_now, tokens), head_columns(g_now, h)] = result[
                    h * tokens : (h + 1) * tokens
                ]

    covered = full + half.astype(jnp.int32)

    @pl.loop(covered, SLOT // TOKENS)
    def _(i):
        token = pl.multiple_of(i * TOKENS, TOKENS)
        result_ref[pl.ds(token, TOKENS), :] = jnp.zeros((TOKENS, GROUPS * HEADS * HEAD), BF16)
        store(token, TOKENS)

    @pl.when(full > 0)
    def _():
        step(TOKENS, None, None, (0, 0), scores_a)

        @pl.loop(0, full - 1)
        def _(i):
            token = i * TOKENS
            step(TOKENS, (0, token), scores_a, (1, token), scores_b)
            step(TOKENS, (1, token), scores_b, (0, token + TOKENS), scores_a)
            store(token, TOKENS)

        token = (full - 1) * TOKENS
        step(TOKENS, (0, token), scores_a, (1, token), scores_b)
        step(TOKENS, (1, token), scores_b, None, None)
        store(token, TOKENS)

    @pl.when(half)
    def _():
        tokens = TOKENS // 2
        token = full * TOKENS
        step(tokens, None, None, (0, token), scores_a)
        step(tokens, (0, token), scores_a, (1, token), scores_b)
        step(tokens, (1, token), scores_b, None, None)
        rest = pl.ds(pl.multiple_of(token + tokens, tokens), tokens)
        result_ref[rest, :] = jnp.zeros((tokens, GROUPS * HEADS * HEAD), BF16)
        store(token, TOKENS)

    pltpu.make_async_copy(result_ref, out.at[1], local.at[1]).wait()
    carry_over.wait()


def second(lengths, queries, own, prompt, done):
    vmem = pltpu.VMEM
    return pl.pallas_call(
        second_kernel,
        in_specs=[pl.BlockSpec(memory_space=pltpu.SMEM)] + [pl.BlockSpec(memory_space=vmem)] * 4,
        out_specs=pl.BlockSpec(memory_space=pltpu.HBM),
        out_shape=jax.ShapeDtypeStruct(queries.shape, BF16),
        scratch_shapes=[
            vmem((ROWS, PROMPT + SLOT), F32),
            vmem((ROWS, PROMPT + SLOT), F32),
            vmem((ROWS, HEAD), F32),
            vmem((SLOT, GROUPS * HEADS * HEAD), BF16),
            pltpu.SemaphoreType.DMA((2,)),
        ],
        compiler_params=pltpu.CompilerParams(vmem_limit_bytes=40 << 20),
    )(lengths, queries, own, prompt, done)


def per_device(queries, trace_kv, lengths, prompt_kv):
    lengths, queries = lengths[:, 0], queries[:, 0]
    arguments = (lengths, prompt_kv, queries, trace_kv[:, 0])
    done, prompt, own = first(*(pltpu.with_memory_space_constraint(a, pltpu.HBM) for a in arguments))
    return second(lengths, queries, own, prompt, done)[:, None]


def solution(mesh):
    placed = (
        P(None, "dp", None, "tensor"),
        P(None, "dp", None, None, "tensor"),
        P(None, "dp"),
        P(("dp", "tensor"), None, None),
    )
    return jax.shard_map(
        per_device,
        mesh=mesh,
        in_specs=placed,
        out_specs=P(None, "dp", None, "tensor"),
        check_vma=False,
    )
```

```python
import math

import jax
import jax.numpy as jnp
from jax import lax
from jax.experimental import pallas as pl
from jax.experimental.pallas import tpu as pltpu
from jax.sharding import PartitionSpec as P

MESH = pl.DeviceIdType.MESH
BF16 = jnp.bfloat16
F32 = jnp.float32
HEAD = 128
HEADS = 8
GROUPS = 2
SLOT = 256
PROMPT = 1024
TILE = 256
TOKENS = 64
ROWS = TOKENS * HEADS
PAIRS = HEADS // 2
SCALE = math.log2(math.e) / math.sqrt(HEAD)
NEG = -1e30
PLANES = ((0, 1), (3, 2))


def turn(index, step):
    return lax.rem(index + step, 4)


def coordinates():
    dp, tensor = lax.axis_index("dp"), lax.axis_index("tensor")
    core = lax.rem(dp, 2)
    z = lax.rem(lax.div(dp, 2), 4)
    x = lax.rem(lax.div(dp, 8), 4)
    y = lax.div(dp, 32) * 2 + tensor
    return x, y, z, core


def device(x, y, z, core):
    return (((lax.div(y, 2) * 4 + x) * 4 + z) * 2 + core, lax.rem(y, 2))


def ring_hops(step):
    return min(step, 4 - step)


def remote(src, dst, send, recv, target):
    return pltpu.make_async_remote_copy(
        src_ref=src, dst_ref=dst, send_sem=send, recv_sem=recv, device_id=target, device_id_type=MESH
    )


def landed(ref, sem):
    pltpu.make_async_copy(ref, ref, sem).wait()


def head_columns(g, head):
    return pl.ds(pl.multiple_of(g * HEADS * HEAD + head * HEAD, HEAD), HEAD)


def first_kernel(
    lengths_hbm, shard_hbm, queries, trace_kv, out_hbm, kv_out, later_out,
    lengths, blocks, kv, shard, stage, q, raw, own, later, out, scores, tops, partial,
    s1, r1, s3, r3, local,
):
    x, y, z, core = coordinates()
    tensor = lax.rem(y, 2)
    partner = device(x, y, z, 1 - core)
    load_shard = pltpu.make_async_copy(shard_hbm, shard, local.at[3])
    load_shard.start()
    away = [(a, b, c) for a in range(4) for b in range(4) for c in range(4) if a or b or c]
    away.sort(key=lambda step: -sum(map(ring_hops, step)))
    rows = [turn(y, b) for b in range(4)]
    row_tensor = [lax.rem(row, 2) for row in rows]
    row_base = [lax.div(row, 2) * 32 for row in rows]
    column_base = [[turn(x, a) * 8 + turn(z, c) * 2 + core for c in range(4)] for a in range(4)]

    def chip(step):
        a, b, c = step
        return row_base[b] + column_base[a][c], row_tensor[b]

    barrier = pltpu.get_barrier_semaphore()
    for step in away:
        pl.semaphore_signal(barrier, inc=1, device_id=chip(step), device_id_type=MESH)
    pl.semaphore_signal(barrier, inc=1, device_id=partner, device_id_type=MESH)
    load_lengths = pltpu.make_async_copy(lengths_hbm, lengths, local.at[6])
    load_lengths.start()
    load_q = pltpu.make_async_copy(queries.at[0], q, local.at[0])
    load_own = pltpu.make_async_copy(trace_kv, raw, local.at[1])
    load_q.start()
    load_own.start()
    load_shard.wait()
    for t in range(2):
        for k in range(2):
            columns = t * 2 * HEAD
            stage[t, k] = jnp.concatenate(
                [shard[:, k, columns : columns + HEAD], shard[:, k, columns + HEAD : columns + 2 * HEAD]], 0
            )
    here = x * 16 + y * 4 + z
    pl.semaphore_wait(barrier, len(away) + 1)
    for k in range(2):
        for step in away:
            block = stage.at[row_tensor[step[1]], k]
            remote(block, blocks.at[core, k, here], s1.at[k], r1.at[k, x], chip(step)).start()
    for k in range(2):
        blocks[core, k, here] = stage[tensor, k]

    def scores_of(g, columns, mask=None):
        for j in range(PAIRS):
            pair = jnp.concatenate([q[:, head_columns(g, 2 * j)], q[:, head_columns(g, 2 * j + 1)]], 0)
            top = None if mask is not None else tops[g * PAIRS + j]
            for column in columns:
                keys = kv[g, column, 0] if column < 4 else own[g, 0]
                tile = lax.dot_general(pair, keys, (((1,), (1,)), ((), ())), preferred_element_type=F32)
                if mask is not None:
                    tile = jnp.where(mask, tile, NEG)
                scores[g * PAIRS + j, :, column * TILE : (column + 1) * TILE] = tile
                tile = jnp.maximum(tile[:, :HEAD], tile[:, HEAD:])
                top = tile if top is None else jnp.maximum(top, tile)
            tops[g * PAIRS + j] = top

    load_own.wait()
    for s, target in ((0, own), (1, later)):
        for g in range(GROUPS):
            for k in range(2):
                target[g, k] = raw[s, :, k, g * HEAD : (g + 1) * HEAD]
    keep_later = pltpu.make_async_copy(later, later_out, local.at[4])
    keep_later.start()
    load_q.wait()
    load_lengths.wait()
    length = lengths[0]
    position = lax.rem(lax.broadcasted_iota(jnp.int32, (2 * SLOT, TILE), 0), SLOT)
    key = lax.broadcasted_iota(jnp.int32, (2 * SLOT, TILE), 1)
    allowed = (key <= position) & (key < length)

    @pl.loop(0, GROUPS)
    def _(g):
        scores_of(g, (4,), allowed)

    def group(side, k, d):
        return blocks.at[side, k, pl.ds(pl.multiple_of(turn(x, d) * 16, 16), 16)]

    def arrange(side, column, k):
        for g in range(GROUPS):
            rows = [group(side, k, d)[:, g * 8 : (g + 1) * 8].reshape(TILE // 2, HEAD) for d in PLANES[column % 2]]
            kv[g, column, k] = jnp.concatenate(rows, 0)

    def collect(k, column):
        for d in PLANES[column]:
            if d:
                landed(group(core, k, d), r1.at[k, turn(x, d)])
            else:
                landed(blocks.at[core, k, 0:15], r1.at[k, x])
            remote(group(core, k, d), group(core, k, d), s3.at[k, d], r3.at[k, d], partner).start()
        arrange(core, column, k)

    def collect_partner(k, column):
        for d in PLANES[column - 2]:
            landed(group(1 - core, k, d), r3.at[k, d])
        arrange(1 - core, column, k)

    for column in (0, 1):
        collect(0, column)

    @pl.loop(0, GROUPS)
    def _(g):
        scores_of(g, (0, 1))

    for column in (2, 3):
        collect_partner(0, column)
    for g in range(GROUPS):
        scores_of(g, (2, 3))
        for pair in range(g * PAIRS, (g + 1) * PAIRS):
            tops[pair] = jnp.broadcast_to(jnp.max(tops[pair], -1, keepdims=True), (2 * SLOT, HEAD))
        if g == 0:
            collect(1, 0)
            collect(1, 1)
    ones = jnp.ones((TILE, HEAD), BF16)

    def attended(step, columns):
        g = lax.div(step, PAIRS // 2)
        totals = [None, None]
        for column in columns:
            values = kv[g, column, 1] if column < 4 else own[g, 1]
            values = jnp.concatenate([values, ones], 1)
            for i in range(2):
                pair = 2 * step + i
                top = jnp.concatenate([tops[pair], tops[pair]], 1)
                tile = scores[pair, :, column * TILE : (column + 1) * TILE]
                weights = jnp.exp2((tile - top) * SCALE).astype(BF16)
                total = jnp.dot(weights, values, preferred_element_type=F32)
                totals[i] = total if totals[i] is None else totals[i] + total
        return totals

    def finish(step, totals):
        results = []
        for total in totals:
            result = total[:, :HEAD] / total[:, HEAD:]
            result = jnp.where(position[:, :HEAD] < length, result, 0.0).astype(BF16)
            results += [result[:SLOT], result[SLOT:]]
        columns = pl.ds(pl.multiple_of(step * 4 * HEAD, 4 * HEAD), 4 * HEAD)
        out[:, columns] = jnp.concatenate(results, 1)
        pltpu.make_async_copy(out.at[:, columns], out_hbm.at[:, columns], local.at[5]).start()

    for i, total in enumerate(attended(0, (4, 0, 1))):
        partial[i] = total
    for column in (2, 3):
        collect_partner(1, column)
    keep = pltpu.make_async_copy(kv, kv_out, local.at[2])
    keep.start()
    finish(0, [partial[i] + total for i, total in enumerate(attended(0, (2, 3)))])

    @pl.loop(1, PAIRS)
    def _(step):
        finish(step, attended(step, (0, 1, 2, 3, 4)))

    keep.wait()
    keep_later.wait()
    landed(out, local.at[5])
    for k in range(2):
        landed(blocks.at[core, k, 0:63], s1.at[k])
        for d in range(4):
            landed(group(core, k, d), s3.at[k, d])


def first(lengths, shard, queries, trace_kv):
    vmem, dma = pltpu.VMEM, pltpu.SemaphoreType.DMA
    gathered = (GROUPS, 4, 2, TILE, HEAD)
    columns = GROUPS * HEADS * HEAD
    own = (GROUPS, 2, SLOT, HEAD)
    return pl.pallas_call(
        first_kernel,
        in_specs=[pl.BlockSpec(memory_space=pltpu.HBM)] * 4,
        out_specs=[pl.BlockSpec(memory_space=pltpu.HBM)] * 3,
        out_shape=[
            jax.ShapeDtypeStruct((SLOT, columns), BF16),
            jax.ShapeDtypeStruct(gathered, BF16),
            jax.ShapeDtypeStruct(own, BF16),
        ],
        scratch_shapes=[
            pltpu.SMEM((2,), jnp.int32),
            vmem((2, 2, 64, 16, HEAD), BF16),
            vmem(gathered, BF16),
            vmem((8, 2, 2 * GROUPS * HEAD), BF16),
            vmem((2, 2, 16, HEAD), BF16),
            vmem((SLOT, columns), BF16),
            vmem((2, SLOT, 2, GROUPS * HEAD), BF16),
            vmem(own, BF16),
            vmem(own, BF16),
            vmem((SLOT, columns), BF16),
            vmem((2 * PAIRS, 2 * SLOT, PROMPT + SLOT), F32),
            vmem((2 * PAIRS, 2 * SLOT, HEAD), F32),
            vmem((2, 2 * SLOT, 2 * HEAD), F32),
            dma((2,)), dma((2, 4)), dma((2, 4)), dma((2, 4)), dma((7,)),
        ],
        compiler_params=pltpu.CompilerParams(
            collective_id=0, has_side_effects=True, vmem_limit_bytes=44 << 20
        ),
    )(lengths, shard, queries, trace_kv)


def second_kernel(lengths, q, own, prompt, done, out, scores_a, scores_b, tops, result_ref, local):
    carry_over = pltpu.make_async_copy(done, out.at[0], local.at[0])
    carry_over.start()
    length = lengths[1]
    full = lax.div(length + TOKENS // 2 - 1, TOKENS)
    half = full * TOKENS < length
    ones = jnp.ones((TILE, HEAD), BF16)

    def store(token, tokens):
        rows = pl.ds(pl.multiple_of(token, tokens), tokens)
        pltpu.make_async_copy(result_ref.at[rows], out.at[1, rows], local.at[1]).start()

    def step(tokens, current, scores_now, following, scores_next):
        rows = tokens * HEADS
        position = lax.rem(lax.broadcasted_iota(jnp.int32, (rows, TILE), 0), tokens)
        if following is not None:
            g, token = following
            token = pl.multiple_of(token, tokens)
            queries = jnp.concatenate(
                [q[1, pl.ds(token, tokens), head_columns(g, h)] for h in range(HEADS)], 0
            )
            part_top = None
        if current is not None:
            g_now, token_now = current
            token_now = pl.multiple_of(token_now, tokens)
            top = tops[:rows]
            top = jnp.concatenate([top, top], 1)
            total = jnp.zeros((rows, 2 * HEAD), F32)
        for k in range(5):
            keys = slice(k * TILE, (k + 1) * TILE)
            if following is not None:
                source = prompt[g, k, 0] if k < 4 else own[g, 0]
                part = lax.dot_general(
                    queries, source, (((1,), (1,)), ((), ())), preferred_element_type=F32
                )
                if k == 4:
                    key = lax.broadcasted_iota(jnp.int32, (rows, TILE), 1)
                    part = jnp.where((key <= position + token) & (key < length), part, NEG)
                scores_next[:rows, keys] = part
                part = jnp.maximum(part[:, :HEAD], part[:, HEAD:])
                part_top = part if part_top is None else jnp.maximum(part_top, part)
            if current is not None:
                weights = jnp.exp2((scores_now[:rows, keys] - top) * SCALE).astype(BF16)
                source = prompt[g_now, k, 1] if k < 4 else own[g_now, 1]
                total += jnp.dot(
                    weights, jnp.concatenate([source, ones], 1), preferred_element_type=F32
                )
        if following is not None:
            tops[:rows] = jnp.broadcast_to(jnp.max(part_top, -1, keepdims=True), (rows, HEAD))
        if current is not None:
            result = total[:, :HEAD] / total[:, HEAD:]
            result = jnp.where(position[:, :HEAD] + token_now < length, result, 0.0).astype(BF16)
            for h in range(HEADS):
                result_ref[pl.ds(token_now, tokens), head_columns(g_now, h)] = result[
                    h * tokens : (h + 1) * tokens
                ]

    covered = full + half.astype(jnp.int32)

    @pl.loop(covered, SLOT // TOKENS)
    def _(i):
        token = pl.multiple_of(i * TOKENS, TOKENS)
        result_ref[pl.ds(token, TOKENS), :] = jnp.zeros((TOKENS, GROUPS * HEADS * HEAD), BF16)
        store(token, TOKENS)

    @pl.when(full > 0)
    def _():
        step(TOKENS, None, None, (0, 0), scores_a)

        @pl.loop(0, full - 1)
        def _(i):
            token = i * TOKENS
            step(TOKENS, (0, token), scores_a, (1, token), scores_b)
            step(TOKENS, (1, token), scores_b, (0, token + TOKENS), scores_a)
            store(token, TOKENS)

        token = (full - 1) * TOKENS
        step(TOKENS, (0, token), scores_a, (1, token), scores_b)
        step(TOKENS, (1, token), scores_b, None, None)
        store(token, TOKENS)

    @pl.when(half)
    def _():
        tokens = TOKENS // 2
        token = full * TOKENS
        step(tokens, None, None, (0, token), scores_a)
        step(tokens, (0, token), scores_a, (1, token), scores_b)
        step(tokens, (1, token), scores_b, None, None)
        rest = pl.ds(pl.multiple_of(token + tokens, tokens), tokens)
        result_ref[rest, :] = jnp.zeros((tokens, GROUPS * HEADS * HEAD), BF16)
        store(token, TOKENS)

    pltpu.make_async_copy(result_ref, out.at[1], local.at[1]).wait()
    carry_over.wait()


def second(lengths, queries, own, prompt, done):
    vmem = pltpu.VMEM
    return pl.pallas_call(
        second_kernel,
        in_specs=[pl.BlockSpec(memory_space=pltpu.SMEM)] + [pl.BlockSpec(memory_space=vmem)] * 4,
        out_specs=pl.BlockSpec(memory_space=pltpu.HBM),
        out_shape=jax.ShapeDtypeStruct(queries.shape, BF16),
        scratch_shapes=[
            vmem((ROWS, PROMPT + SLOT), F32),
            vmem((ROWS, PROMPT + SLOT), F32),
            vmem((ROWS, HEAD), F32),
            vmem((SLOT, GROUPS * HEADS * HEAD), BF16),
            pltpu.SemaphoreType.DMA((2,)),
        ],
        compiler_params=pltpu.CompilerParams(vmem_limit_bytes=40 << 20),
    )(lengths, queries, own, prompt, done)


def per_device(queries, trace_kv, lengths, prompt_kv):
    lengths, queries = lengths[:, 0], queries[:, 0]
    arguments = (lengths, prompt_kv, queries, trace_kv[:, 0])
    done, prompt, own = first(*(pltpu.with_memory_space_constraint(a, pltpu.HBM) for a in arguments))
    return second(lengths, queries, own, prompt, done)[:, None]


def solution(mesh):
    placed = (
        P(None, "dp", None, "tensor"),
        P(None, "dp", None, None, "tensor"),
        P(None, "dp"),
        P(("dp", "tensor"), None, None),
    )
    return jax.shard_map(
        per_device,
        mesh=mesh,
        in_specs=placed,
        out_specs=P(None, "dp", None, "tensor"),
        check_vma=False,
    )
```

```python
import math

import jax
import jax.numpy as jnp
from jax import lax
from jax.experimental import pallas as pl
from jax.experimental.pallas import tpu as pltpu
from jax.sharding import PartitionSpec as P

MESH = pl.DeviceIdType.MESH
BF16 = jnp.bfloat16
F32 = jnp.float32
HEAD = 128
HEADS = 8
GROUPS = 2
SLOT = 256
PROMPT = 1024
TILE = 256
TOKENS = 64
ROWS = TOKENS * HEADS
PAIRS = HEADS // 2
SCALE = math.log2(math.e) / math.sqrt(HEAD)
NEG = -1e30
PLANES = ((0, 1), (3, 2))


def turn(index, step):
    return lax.rem(index + step, 4)


def coordinates():
    dp, tensor = lax.axis_index("dp"), lax.axis_index("tensor")
    core = lax.rem(dp, 2)
    z = lax.rem(lax.div(dp, 2), 4)
    x = lax.rem(lax.div(dp, 8), 4)
    y = lax.div(dp, 32) * 2 + tensor
    return x, y, z, core


def device(x, y, z, core):
    return (((lax.div(y, 2) * 4 + x) * 4 + z) * 2 + core, lax.rem(y, 2))


def ring_hops(step):
    return min(step, 4 - step)


def remote(src, dst, send, recv, target):
    return pltpu.make_async_remote_copy(
        src_ref=src, dst_ref=dst, send_sem=send, recv_sem=recv, device_id=target, device_id_type=MESH
    )


def landed(ref, sem):
    pltpu.make_async_copy(ref, ref, sem).wait()


def head_columns(g, head):
    return pl.ds(pl.multiple_of(g * HEADS * HEAD + head * HEAD, HEAD), HEAD)


def first_kernel(
    lengths_hbm, shard_hbm, queries, trace_kv, out_hbm, kv_out, later_out,
    lengths, blocks, kv, shard, stage, q, raw, own, later, out, scores, tops, partial,
    s1, r1, s3, r3, local,
):
    x, y, z, core = coordinates()
    tensor = lax.rem(y, 2)
    partner = device(x, y, z, 1 - core)
    load_shard = pltpu.make_async_copy(shard_hbm, shard, local.at[3])
    load_shard.start()
    away = [(a, b, c) for a in range(4) for b in range(4) for c in range(4) if a or b or c]
    away.sort(key=lambda step: -sum(map(ring_hops, step)))
    rows = [turn(y, b) for b in range(4)]
    row_tensor = [lax.rem(row, 2) for row in rows]
    row_base = [lax.div(row, 2) * 32 for row in rows]
    column_base = [[turn(x, a) * 8 + turn(z, c) * 2 + core for c in range(4)] for a in range(4)]

    def chip(step):
        a, b, c = step
        return row_base[b] + column_base[a][c], row_tensor[b]

    barrier = pltpu.get_barrier_semaphore()
    for step in away:
        pl.semaphore_signal(barrier, inc=1, device_id=chip(step), device_id_type=MESH)
    pl.semaphore_signal(barrier, inc=1, device_id=partner, device_id_type=MESH)
    load_lengths = pltpu.make_async_copy(lengths_hbm, lengths, local.at[6])
    load_lengths.start()
    load_q = pltpu.make_async_copy(queries.at[0], q, local.at[0])
    load_own = pltpu.make_async_copy(trace_kv, raw, local.at[1])
    load_q.start()
    load_own.start()
    load_shard.wait()
    for t in range(2):
        for k in range(2):
            columns = t * 2 * HEAD
            stage[t, k] = jnp.concatenate(
                [shard[:, k, columns : columns + HEAD], shard[:, k, columns + HEAD : columns + 2 * HEAD]], 0
            )
    here = x * 16 + y * 4 + z
    pl.semaphore_wait(barrier, len(away) + 1)
    for k in range(2):
        for step in away:
            block = stage.at[row_tensor[step[1]], k]
            remote(block, blocks.at[core, k, here], s1.at[k], r1.at[k, x], chip(step)).start()
    for k in range(2):
        blocks[core, k, here] = stage[tensor, k]

    def scores_of(g, columns, mask=None):
        for j in range(PAIRS):
            pair = jnp.concatenate([q[:, head_columns(g, 2 * j)], q[:, head_columns(g, 2 * j + 1)]], 0)
            top = None if mask is not None else tops[g * PAIRS + j]
            for column in columns:
                keys = kv[g, column, 0] if column < 4 else own[g, 0]
                tile = lax.dot_general(pair, keys, (((1,), (1,)), ((), ())), preferred_element_type=F32)
                if mask is not None:
                    tile = jnp.where(mask, tile, NEG)
                scores[g * PAIRS + j, :, column * TILE : (column + 1) * TILE] = tile
                tile = jnp.maximum(tile[:, :HEAD], tile[:, HEAD:])
                top = tile if top is None else jnp.maximum(top, tile)
            tops[g * PAIRS + j] = top

    load_own.wait()
    for s, target in ((0, own), (1, later)):
        for g in range(GROUPS):
            for k in range(2):
                target[g, k] = raw[s, :, k, g * HEAD : (g + 1) * HEAD]
    keep_later = pltpu.make_async_copy(later, later_out, local.at[4])
    keep_later.start()
    load_q.wait()
    load_lengths.wait()
    length = lengths[0]
    position = lax.rem(lax.broadcasted_iota(jnp.int32, (2 * SLOT, TILE), 0), SLOT)
    key = lax.broadcasted_iota(jnp.int32, (2 * SLOT, TILE), 1)
    allowed = (key <= position) & (key < length)

    @pl.loop(0, GROUPS)
    def _(g):
        scores_of(g, (4,), allowed)

    def group(side, k, d):
        return blocks.at[side, k, pl.ds(pl.multiple_of(turn(x, d) * 16, 16), 16)]

    def arrange(side, column, k):
        for g in range(GROUPS):
            rows = [group(side, k, d)[:, g * 8 : (g + 1) * 8].reshape(TILE // 2, HEAD) for d in PLANES[column % 2]]
            kv[g, column, k] = jnp.concatenate(rows, 0)

    def collect(k, column):
        for d in PLANES[column]:
            if d:
                landed(group(core, k, d), r1.at[k, turn(x, d)])
            else:
                landed(blocks.at[core, k, 0:15], r1.at[k, x])
            remote(group(core, k, d), group(core, k, d), s3.at[k, d], r3.at[k, d], partner).start()
        arrange(core, column, k)

    def collect_partner(k, column):
        for d in PLANES[column - 2]:
            landed(group(1 - core, k, d), r3.at[k, d])
        arrange(1 - core, column, k)

    for column in (0, 1):
        collect(0, column)

    for g in range(GROUPS):
        scores_of(g, (0, 1))

    for column in (2, 3):
        collect_partner(0, column)
    for g in range(GROUPS):
        scores_of(g, (2, 3))
        for pair in range(g * PAIRS, (g + 1) * PAIRS):
            tops[pair] = jnp.broadcast_to(jnp.max(tops[pair], -1, keepdims=True), (2 * SLOT, HEAD))
        if g == 0:
            collect(1, 0)
            collect(1, 1)
    ones = jnp.ones((TILE, HEAD), BF16)

    def attended(step, columns):
        g = lax.div(step, PAIRS // 2)
        totals = [None, None]
        for column in columns:
            values = kv[g, column, 1] if column < 4 else own[g, 1]
            values = jnp.concatenate([values, ones], 1)
            for i in range(2):
                pair = 2 * step + i
                top = jnp.concatenate([tops[pair], tops[pair]], 1)
                tile = scores[pair, :, column * TILE : (column + 1) * TILE]
                weights = jnp.exp2((tile - top) * SCALE).astype(BF16)
                total = jnp.dot(weights, values, preferred_element_type=F32)
                totals[i] = total if totals[i] is None else totals[i] + total
        return totals

    def finish(step, totals):
        results = []
        for total in totals:
            result = total[:, :HEAD] / total[:, HEAD:]
            result = jnp.where(position[:, :HEAD] < length, result, 0.0).astype(BF16)
            results += [result[:SLOT], result[SLOT:]]
        columns = pl.ds(pl.multiple_of(step * 4 * HEAD, 4 * HEAD), 4 * HEAD)
        out[:, columns] = jnp.concatenate(results, 1)
        pltpu.make_async_copy(out.at[:, columns], out_hbm.at[:, columns], local.at[5]).start()

    for i, total in enumerate(attended(0, (4, 0, 1))):
        partial[i] = total
    for column in (2, 3):
        collect_partner(1, column)
    keep = pltpu.make_async_copy(kv, kv_out, local.at[2])
    keep.start()
    finish(0, [partial[i] + total for i, total in enumerate(attended(0, (2, 3)))])

    @pl.loop(1, PAIRS)
    def _(step):
        finish(step, attended(step, (0, 1, 2, 3, 4)))

    keep.wait()
    keep_later.wait()
    landed(out, local.at[5])
    for k in range(2):
        landed(blocks.at[core, k, 0:63], s1.at[k])
        for d in range(4):
            landed(group(core, k, d), s3.at[k, d])


def first(lengths, shard, queries, trace_kv):
    vmem, dma = pltpu.VMEM, pltpu.SemaphoreType.DMA
    gathered = (GROUPS, 4, 2, TILE, HEAD)
    columns = GROUPS * HEADS * HEAD
    own = (GROUPS, 2, SLOT, HEAD)
    return pl.pallas_call(
        first_kernel,
        in_specs=[pl.BlockSpec(memory_space=pltpu.HBM)] * 4,
        out_specs=[pl.BlockSpec(memory_space=pltpu.HBM)] * 3,
        out_shape=[
            jax.ShapeDtypeStruct((SLOT, columns), BF16),
            jax.ShapeDtypeStruct(gathered, BF16),
            jax.ShapeDtypeStruct(own, BF16),
        ],
        scratch_shapes=[
            pltpu.SMEM((2,), jnp.int32),
            vmem((2, 2, 64, 16, HEAD), BF16),
            vmem(gathered, BF16),
            vmem((8, 2, 2 * GROUPS * HEAD), BF16),
            vmem((2, 2, 16, HEAD), BF16),
            vmem((SLOT, columns), BF16),
            vmem((2, SLOT, 2, GROUPS * HEAD), BF16),
            vmem(own, BF16),
            vmem(own, BF16),
            vmem((SLOT, columns), BF16),
            vmem((2 * PAIRS, 2 * SLOT, PROMPT + SLOT), F32),
            vmem((2 * PAIRS, 2 * SLOT, HEAD), F32),
            vmem((2, 2 * SLOT, 2 * HEAD), F32),
            dma((2,)), dma((2, 4)), dma((2, 4)), dma((2, 4)), dma((7,)),
        ],
        compiler_params=pltpu.CompilerParams(
            collective_id=0, has_side_effects=True, vmem_limit_bytes=44 << 20
        ),
    )(lengths, shard, queries, trace_kv)


def second_kernel(lengths, q, own, prompt, done, out, scores_a, scores_b, tops, result_ref, local):
    carry_over = pltpu.make_async_copy(done, out.at[0], local.at[0])
    carry_over.start()
    length = lengths[1]
    full = lax.div(length + TOKENS // 2 - 1, TOKENS)
    half = full * TOKENS < length
    ones = jnp.ones((TILE, HEAD), BF16)

    def store(token, tokens):
        rows = pl.ds(pl.multiple_of(token, tokens), tokens)
        pltpu.make_async_copy(result_ref.at[rows], out.at[1, rows], local.at[1]).start()

    def step(tokens, current, scores_now, following, scores_next):
        rows = tokens * HEADS
        position = lax.rem(lax.broadcasted_iota(jnp.int32, (rows, TILE), 0), tokens)
        if following is not None:
            g, token = following
            token = pl.multiple_of(token, tokens)
            queries = jnp.concatenate(
                [q[1, pl.ds(token, tokens), head_columns(g, h)] for h in range(HEADS)], 0
            )
            part_top = None
        if current is not None:
            g_now, token_now = current
            token_now = pl.multiple_of(token_now, tokens)
            top = tops[:rows]
            top = jnp.concatenate([top, top], 1)
            total = jnp.zeros((rows, 2 * HEAD), F32)
        for k in range(5):
            keys = slice(k * TILE, (k + 1) * TILE)
            if following is not None:
                source = prompt[g, k, 0] if k < 4 else own[g, 0]
                part = lax.dot_general(
                    queries, source, (((1,), (1,)), ((), ())), preferred_element_type=F32
                )
                if k == 4:
                    key = lax.broadcasted_iota(jnp.int32, (rows, TILE), 1)
                    part = jnp.where((key <= position + token) & (key < length), part, NEG)
                scores_next[:rows, keys] = part
                part = jnp.maximum(part[:, :HEAD], part[:, HEAD:])
                part_top = part if part_top is None else jnp.maximum(part_top, part)
            if current is not None:
                weights = jnp.exp2((scores_now[:rows, keys] - top) * SCALE).astype(BF16)
                source = prompt[g_now, k, 1] if k < 4 else own[g_now, 1]
                total += jnp.dot(
                    weights, jnp.concatenate([source, ones], 1), preferred_element_type=F32
                )
        if following is not None:
            tops[:rows] = jnp.broadcast_to(jnp.max(part_top, -1, keepdims=True), (rows, HEAD))
        if current is not None:
            result = total[:, :HEAD] / total[:, HEAD:]
            result = jnp.where(position[:, :HEAD] + token_now < length, result, 0.0).astype(BF16)
            for h in range(HEADS):
                result_ref[pl.ds(token_now, tokens), head_columns(g_now, h)] = result[
                    h * tokens : (h + 1) * tokens
                ]

    covered = full + half.astype(jnp.int32)

    @pl.loop(covered, SLOT // TOKENS)
    def _(i):
        token = pl.multiple_of(i * TOKENS, TOKENS)
        result_ref[pl.ds(token, TOKENS), :] = jnp.zeros((TOKENS, GROUPS * HEADS * HEAD), BF16)
        store(token, TOKENS)

    @pl.when(full > 0)
    def _():
        step(TOKENS, None, None, (0, 0), scores_a)

        @pl.loop(0, full - 1)
        def _(i):
            token = i * TOKENS
            step(TOKENS, (0, token), scores_a, (1, token), scores_b)
            step(TOKENS, (1, token), scores_b, (0, token + TOKENS), scores_a)
            store(token, TOKENS)

        token = (full - 1) * TOKENS
        step(TOKENS, (0, token), scores_a, (1, token), scores_b)
        step(TOKENS, (1, token), scores_b, None, None)
        store(token, TOKENS)

    @pl.when(half)
    def _():
        tokens = TOKENS // 2
        token = full * TOKENS
        step(tokens, None, None, (0, token), scores_a)
        step(tokens, (0, token), scores_a, (1, token), scores_b)
        step(tokens, (1, token), scores_b, None, None)
        rest = pl.ds(pl.multiple_of(token + tokens, tokens), tokens)
        result_ref[rest, :] = jnp.zeros((tokens, GROUPS * HEADS * HEAD), BF16)
        store(token, TOKENS)

    pltpu.make_async_copy(result_ref, out.at[1], local.at[1]).wait()
    carry_over.wait()


def second(lengths, queries, own, prompt, done):
    vmem = pltpu.VMEM
    return pl.pallas_call(
        second_kernel,
        in_specs=[pl.BlockSpec(memory_space=pltpu.SMEM)] + [pl.BlockSpec(memory_space=vmem)] * 4,
        out_specs=pl.BlockSpec(memory_space=pltpu.HBM),
        out_shape=jax.ShapeDtypeStruct(queries.shape, BF16),
        scratch_shapes=[
            vmem((ROWS, PROMPT + SLOT), F32),
            vmem((ROWS, PROMPT + SLOT), F32),
            vmem((ROWS, HEAD), F32),
            vmem((SLOT, GROUPS * HEADS * HEAD), BF16),
            pltpu.SemaphoreType.DMA((2,)),
        ],
        compiler_params=pltpu.CompilerParams(vmem_limit_bytes=40 << 20),
    )(lengths, queries, own, prompt, done)


def per_device(queries, trace_kv, lengths, prompt_kv):
    lengths, queries = lengths[:, 0], queries[:, 0]
    arguments = (lengths, prompt_kv, queries, trace_kv[:, 0])
    done, prompt, own = first(*(pltpu.with_memory_space_constraint(a, pltpu.HBM) for a in arguments))
    return second(lengths, queries, own, prompt, done)[:, None]


def solution(mesh):
    placed = (
        P(None, "dp", None, "tensor"),
        P(None, "dp", None, None, "tensor"),
        P(None, "dp"),
        P(("dp", "tensor"), None, None),
    )
    return jax.shard_map(
        per_device,
        mesh=mesh,
        in_specs=placed,
        out_specs=P(None, "dp", None, "tensor"),
        check_vma=False,
    )
```
